32 devices in a mesh: frame: 4 (over x, core), row: 8 (over z, y).
Axes of the slice: x: 2, y: 2, z: 4, core: 2. Of those that a mesh axis runs over, the one named last changes fastest.
Arguments:
- queries: bfloat16 [4, 64, 16, 1536], P('frame', 'row'), may hold values from -128 to 128
- keys: bfloat16 [4, 64, 16, 1536], P('frame', 'row'), may hold values from -6 to 6
- values: bfloat16 [4, 64, 16, 1536], P('frame', 'row'), may hold values from -6 to 6
- window_mask: int32 [4, 8, 2, 45], P('frame', 'row'), may hold values 0 or 1
- tile_valid: int32 [4, 8, 2], replicated, may hold values 0 or 1
- w_out: bfloat16 [1536, 3072], replicated, may hold values from -0.5 to 0.5
- gate: float32 [3072], replicated, may hold values from 0.5 to 4
Outputs:
- update: bfloat16 [4, 64, 16, 3072], P('frame', 'row')
The draws below stay inside these ranges and needn't reach their ends.
All inputs are finite; a program needn't handle non-finite values. No bound on the sum of `window_mask` on one device may be relied on, other than what follows from the above.
Results may differ from the reference program's by a relative error of at most 0.0053.
Values may be sent and summed in bfloat16 or wider, within the bound.
A program may use at most 128 MiB of HBM per device.

```python
import math
import jax
import jax.numpy as jnp
from jax import lax

D = 3072
HEADS = 12
HD = 128
FR_TILE = 1
ROW_TILE = 8
COL_TILE = 8
OFFSETS = 45
WID = 16
FRAMES = 4
ROWS = 64
COL_TILES = 2
N_FRAME = 4
N_ROW = 8


def pair_draw(key):
    grid_shape = (FR_TILE * N_FRAME, ROW_TILE * N_ROW, WID, HEADS * HD)
    key_query = jax.random.fold_in(key, 101)
    key_keys = jax.random.fold_in(key, 202)
    query_base = 2.0 * jnp.clip(jax.random.normal(key_query, grid_shape, jnp.float32), -6.0, 6.0)
    key_base = jnp.clip(jax.random.normal(key_keys, grid_shape, jnp.float32), -6.0, 6.0)
    return (query_base, key_base)


def draw_queries(key, part):
    return pair_draw(key)[0].astype(jnp.bfloat16)


def draw_keys(key, part):
    return pair_draw(key)[1].astype(jnp.bfloat16)


def set_ends(entries, own_key, smallest, largest):
    index_at = [jax.random.randint(jax.random.fold_in(own_key, axis), (), 0, length) for axis, length in enumerate(entries.shape)]
    longest = entries.shape.index(max(entries.shape))
    neighbour = index_at[:longest] + [(index_at[longest] + 1) % entries.shape[longest]] + index_at[longest + 1:]
    return entries.at[tuple(index_at)].set(smallest).at[tuple(neighbour)].set(largest)


def levels(stream_key, shape, split, least, largest):
    gain, own = 1.0, jax.random.fold_in(stream_key, 6)
    for dim, shards_of in split:
        heights = jnp.exp(jax.random.uniform(jax.random.fold_in(own, dim), (shards_of,), jnp.float32, least / len(split), largest / len(split)))
        gain = gain * jnp.repeat(heights, shape[dim] // shards_of).reshape([-1 if axis == dim else 1 for axis in range(len(shape))])
    return gain


def bell_draw(key, extent, spread, bound, pieces=(), kind=jnp.bfloat16):
    factor_of = levels(key, extent, pieces, -0.22, 0.18) if pieces else 1.0
    values = jax.random.normal(key, extent, jnp.float32) * spread * factor_of
    return jnp.minimum(jnp.maximum(values, -bound), bound).astype(kind)


def setup_inputs(seed: int = 0) -> dict:
    splits = jax.random.split(jax.random.key(seed), 8)
    return {
        "queries": draw_queries(jax.random.fold_in(splits[7], 71), 0),
        "keys": draw_keys(jax.random.fold_in(splits[7], 71), 0),
        "values": bell_draw(splits[2], (FRAMES, ROWS, WID, HEADS * HD), 1.0, 6.0, ((0, 4), (1, 8))),
        "window_mask": set_ends((jax.random.randint(splits[3], (N_FRAME, N_ROW, COL_TILES, OFFSETS), 0, 4) < 3).astype(jnp.int32), jax.random.fold_in(splits[3], 1), 0, 1),
        "tile_valid": set_ends((jax.random.randint(splits[4], (N_FRAME, N_ROW, COL_TILES), 0, 6) < 5).astype(jnp.int32), jax.random.fold_in(splits[4], 1), 0, 1),
        "w_out": bell_draw(splits[5], (HEADS * HD, D), HD ** -0.5, 0.5),
        "gate": jnp.clip(jnp.exp(jax.random.uniform(splits[6], (D,), jnp.float32, math.log(0.5), math.log(4.0))), 0.5, 4.0),
    }


def tile_usage(offset_mask, tile_flags):
    col_tiles = offset_mask.shape[0]
    window_table = offset_mask.reshape(col_tiles, 3, 5, 3) == 1
    inside = tile_flags[:, :, 1:col_tiles + 1] == 1
    query_col = jnp.arange(col_tiles)[:, None]
    key_col = jnp.arange(col_tiles)[None, :]
    centre = (jnp.arange(3)[:, None] == 1) & (jnp.arange(5)[None, :] == 2)
    usable = jnp.zeros((col_tiles, 3, 5, col_tiles), dtype=bool)
    for shift_col in (-1, 0, 1):
        col_pair = key_col - query_col == shift_col
        allowed = window_table[:, :, :, shift_col + 1][:, :, :, None] & inside[None]
        if shift_col == 0:
            allowed = allowed | centre[None, :, :, None]
        usable = usable | col_pair[:, None, None, :] & allowed
    return usable

def attend_block(queries, key_ext, value_ext, usable, w_out, gate):
    frames, rows_here, columns, width = queries.shape
    col_tiles = usable.shape[0]
    tile_w = columns // col_tiles
    tok_count = frames * rows_here * columns
    key_count = key_ext.shape[0] * key_ext.shape[1] * columns
    key_mask = jnp.broadcast_to(usable.reshape(1, 1, col_tiles, 1, 3, 1, 5, 1, col_tiles, 1), (frames, rows_here, col_tiles, tile_w, 3, frames, 5, rows_here, col_tiles, tile_w)).reshape(tok_count, key_count)
    flat_query = queries.reshape(tok_count, width)
    flat_key = key_ext.reshape(key_count, width)
    flat_value = value_ext.reshape(key_count, width)
    score_scale = 1.0 / math.sqrt(HD)

    def one_head(head_id):
        start = (head_id * HD).astype(jnp.int32)
        query_head = lax.dynamic_slice_in_dim(flat_query, start, HD, 1)
        key_head = lax.dynamic_slice_in_dim(flat_key, start, HD, 1)
        value_head = lax.dynamic_slice_in_dim(flat_value, start, HD, 1)
        scores = jnp.dot(query_head, key_head.T, preferred_element_type=jnp.float32) * score_scale
        scores = jnp.where(key_mask, scores, -1e+30)
        highest = lax.optimization_barrier(jnp.max(scores, axis=1, keepdims=True))
        weights = jnp.where(key_mask, jnp.exp(scores - highest), 0.0)
        totals = lax.optimization_barrier(jnp.sum(weights, axis=1, keepdims=True))
        mixed = jnp.dot(weights.astype(jnp.bfloat16), value_head, preferred_element_type=jnp.float32)
        return mixed / totals
    head_outs = lax.map(one_head, jnp.arange(HEADS, dtype=jnp.int32))
    attention = head_outs.transpose(1, 0, 2).reshape(tok_count, width).astype(jnp.bfloat16)
    update = jnp.dot(attention, w_out, preferred_element_type=jnp.float32) * gate[None, :]
    return update.astype(jnp.bfloat16).reshape(frames, rows_here, columns, w_out.shape[1])

def reference(queries, keys, values, window_mask, tile_valid, w_out, gate):
    pad_spec = ((FR_TILE, FR_TILE), (2 * ROW_TILE, 2 * ROW_TILE), (0, 0), (0, 0))
    padded_keys = jnp.pad(keys, pad_spec)
    padded_values = jnp.pad(values, pad_spec)
    padded_flags = jnp.pad(tile_valid, ((1, 1), (2, 2), (1, 1)))
    col_tiles = WID // COL_TILE
    zero = jnp.int32(0)

    def one_block(block_id):
        block_id = block_id.astype(jnp.int32)
        frame_idx = (block_id // N_ROW).astype(jnp.int32)
        row_idx = (block_id % N_ROW).astype(jnp.int32)
        start_frame = (frame_idx * FR_TILE).astype(jnp.int32)
        start_row = (row_idx * ROW_TILE).astype(jnp.int32)
        query_block = lax.dynamic_slice(queries, (start_frame, start_row, zero, zero), (FR_TILE, ROW_TILE, WID, HEADS * HD))
        key_block = lax.dynamic_slice(padded_keys, (start_frame, start_row, zero, zero), (3 * FR_TILE, 5 * ROW_TILE, WID, HEADS * HD))
        value_block = lax.dynamic_slice(padded_values, (start_frame, start_row, zero, zero), (3 * FR_TILE, 5 * ROW_TILE, WID, HEADS * HD))
        tile_flags = lax.dynamic_slice(padded_flags, (frame_idx, row_idx, zero), (3, 5, col_tiles + 2))
        offset_mask = lax.dynamic_slice(window_mask, (frame_idx, row_idx, zero, zero), (1, 1, col_tiles, OFFSETS))[0, 0]
        usable = tile_usage(offset_mask, tile_flags)
        return attend_block(query_block, key_block, value_block, usable, w_out, gate)
    blocks = lax.map(one_block, jnp.arange(N_FRAME * N_ROW, dtype=jnp.int32))
    blocks = blocks.reshape(N_FRAME, N_ROW, FR_TILE, ROW_TILE, WID, D)
    return blocks.transpose(0, 2, 1, 3, 4, 5).reshape(N_FRAME * FR_TILE, N_ROW * ROW_TILE, WID, D)
```

```python
import functools
import math

import jax
import jax.numpy as jnp
from jax import lax
from jax.experimental import pallas as pl
from jax.experimental.pallas import tpu as pltpu
from jax.sharding import PartitionSpec as P

HD = 128
FLOOR = -1e20
BLOCKED = -1e30
MESH = pl.DeviceIdType.MESH
GROUPS = 4


def kernel(
    nf, nr, groups,
    q_hbm, k_hbm, v_hbm, wm, tv, w_hbm, gate_ref, out_ref,
    k3, v3, vt, qb, bias_own, bias_in, bias_y, o_out, o_in, own, lse_own,
    y_out, y_in, w_v, acc,
    kv_s, kv_r, qy_s, qy_r, qf_s, qf_r, of_s, of_r, oy_s, oy_r,
    by_s, by_r, bf_s, bf_r, loc, wloc,
):
    tok = q_hbm.shape[0]
    width = q_hbm.shape[1]
    gw = width // groups
    gh = gw // HD
    col_tiles = wm.shape[2]
    f = lax.axis_index("frame")
    r = lax.axis_index("row")
    y = r % 2
    ry = r + 1 - 2 * y
    f_has = (f < nf - 1, f > 0)
    f_dev = ((f + 1, r), (f - 1, r))
    r_has = (r + 2 < nr, r >= 2)
    r_dev = ((f, r + 2), (f, r - 2))
    land = (tok * (2 - y), tok * (1 + y))
    came = (1, 0)
    scale = math.log2(math.e) / math.sqrt(HD)

    barrier = pltpu.get_barrier_semaphore()
    pl.semaphore_signal(barrier, inc=1, device_id=(f, ry), device_id_type=MESH)
    for has, dev in zip(f_has + r_has, f_dev + r_dev):
        @pl.when(has)
        def _(dev=dev):
            pl.semaphore_signal(barrier, inc=1, device_id=dev, device_id_type=MESH)

    locals_ = [
        pltpu.make_async_copy(q_hbm, qb.at[0, 1], loc.at[0]),
        pltpu.make_async_copy(k_hbm, k3.at[pl.ds(0, tok)], loc.at[1]),
        pltpu.make_async_copy(v_hbm, v3.at[pl.ds(0, tok)], loc.at[2]),
    ]
    for c in locals_:
        c.start()

    def cols(g):
        return pl.ds(pl.multiple_of(g * gw, gw), gw)

    def remote(src, dst, s, d, dev):
        return pltpu.make_async_remote_copy(
            src_ref=src, dst_ref=dst, send_sem=s, recv_sem=d,
            device_id=dev, device_id_type=MESH)

    def kv_copy(way, which, g):
        src = (k_hbm, v_hbm)[which]
        dst = (k3, v3)[which]
        rows = pl.ds(pl.multiple_of(land[way], tok), tok)
        return remote(src.at[:, cols(g)], dst.at[rows, cols(g)],
                      kv_s.at[way, which, g], kv_r.at[way, which, g], r_dev[way])

    def qy_copy(g):
        return remote(q_hbm.at[:, cols(g)], qb.at[1, 1, :, cols(g)],
                      qy_s.at[g], qy_r.at[g], (f, ry))

    def qf_copy(way, p, g):
        src = q_hbm.at[:, cols(g)] if p == 0 else qb.at[1, 1, :, cols(g)]
        return remote(src, qb.at[p, 2 * way, :, cols(g)],
                      qf_s.at[way, p, g], qf_r.at[way, p, g], f_dev[way])

    def of_copy(way, p, g):
        return remote(o_out.at[way, p, g], o_in.at[way, p, g],
                      of_s.at[way, p, g], of_r.at[way, p, g], f_dev[way])

    def oy_copy(g):
        return remote(y_out.at[g], y_in.at[g], oy_s.at[g], oy_r.at[g], (f, ry))

    def by_copy():
        return remote(bias_own.at[1], bias_y, by_s, by_r, (f, ry))

    def bf_copy(way, p):
        at = 2 - 2 * way
        src = bias_own.at[0, at] if p == 0 else bias_y.at[at]
        return remote(src, bias_in.at[p, way], bf_s.at[way, p], bf_r.at[way, p], f_dev[way])

    lane_col = (lax.broadcasted_iota(jnp.int32, (1, tok), 1) // 8) % col_tiles
    row8 = lax.broadcasted_iota(jnp.int32, (8, tok), 0)
    row_of = (
        (2, 4 - 4 * y, 4 * y),
        (3 - 2 * y, 1 + 2 * y),
    )
    for p in range(2):
        for df in range(3):
            block = jnp.zeros((8, tok), jnp.float32)
            for slot, dr in enumerate(row_of[p]):
                kf = f + df - 1
                kr = r + dr - 2
                inside = jnp.logical_and(
                    jnp.logical_and(kf >= 0, kf < nf), jnp.logical_and(kr >= 0, kr < nr))
                kfc = jnp.clip(kf, 0, nf - 1)
                krc = jnp.clip(kr, 0, nr - 1)
                for kc in range(col_tiles):
                    valid = jnp.where(inside, tv[kfc, krc, kc], 0)
                    line = jnp.full((1, tok), BLOCKED, jnp.float32)
                    for qc in range(col_tiles):
                        ds = kc - qc
                        if abs(ds) > 1:
                            continue
                        if p == 0 and df == 1 and slot == 0 and ds == 0:
                            val = jnp.float32(0.0)
                        else:
                            o = 15 * df + 3 * dr + ds + 1
                            ok = jnp.where(wm[0, 0, qc, o] == 1, valid, 0)
                            val = jnp.where(ok == 1, 0.0, BLOCKED).astype(jnp.float32)
                        line = jnp.where(lane_col == qc, val, line)
                    block = jnp.where(row8 == slot * col_tiles + kc, line, block)
            bias_own[p, df] = block

    for way in range(2):
        @pl.when(jnp.logical_not(r_has[came[way]]))
        def _(way=way):
            rows = pl.ds(pl.multiple_of(land[way], tok), tok)
            k3[rows, :] = jnp.zeros((tok, width), k3.dtype)
            v3[rows, :] = jnp.zeros((tok, width), v3.dtype)

        @pl.when(jnp.logical_not(f_has[came[way]]))
        def _(way=way):
            lines = o_in.shape[3]
            first = lax.broadcasted_iota(jnp.int32, (lines, tok), 0)
            fill = jnp.where(
                jnp.logical_and(first >= gw, first < gw + gh), FLOOR, 0.0).astype(o_in.dtype)
            for p in range(2):
                for g in range(groups):
                    o_in[way, p, g] = fill

    count = 1 + sum(h.astype(jnp.int32) for h in f_has + r_has)
    pl.semaphore_wait(barrier, count)

    by_copy().start()
    for way in range(2):
        @pl.when(f_has[way])
        def _(way=way):
            bf_copy(way, 0).start()

    @pl.loop(0, groups)
    def _(g):
        qy_copy(g).start()
        for way in range(2):
            @pl.when(f_has[way])
            def _(way=way):
                qf_copy(way, 0, g).start()

            @pl.when(r_has[way])
            def _(way=way):
                kv_copy(way, 0, g).start()
                kv_copy(way, 1, g).start()

    w_copy = pltpu.make_async_copy(w_hbm, w_v, wloc)
    w_copy.start()

    by_copy().wait_recv()
    for way in range(2):
        @pl.when(f_has[way])
        def _(way=way):
            bf_copy(way, 1).start()

        @pl.when(f_has[came[way]])
        def _(way=way):
            bf_copy(way, 0).wait_recv()

    def pass_on(g):
        qy_copy(g).wait_recv()
        for way in range(2):
            @pl.when(f_has[way])
            def _(way=way):
                qf_copy(way, 1, g).start()

    pass_on(0)
    for c in locals_:
        c.wait()
    for way in range(2):
        @pl.when(f_has[came[way]])
        def _(way=way):
            bf_copy(way, 1).wait_recv()

    slots = k3.shape[0] // tok

    def attend(p, d, h, g, bias):
        n_slot = slots - p
        n = n_slot * tok
        at = pl.ds(pl.multiple_of(g * gw + h * HD, HD), HD)
        s = lax.dot_general(
            k3[pl.ds(0, n), at], qb[p, d, :, at], (((1,), (1,)), ((), ())),
            preferred_element_type=jnp.float32)
        s = s * scale
        s = s.reshape(n_slot, tok // (8 * col_tiles), col_tiles, 8, tok)
        s = s + bias[: n_slot * col_tiles].reshape(n_slot, 1, col_tiles, 1, tok)
        s = s.reshape(n, tok)
        m = jnp.maximum(jnp.max(s, axis=0, keepdims=True), FLOOR)
        e = jnp.exp2(s - m)
        total = jnp.sum(e, axis=0, keepdims=True)
        o = jnp.dot(vt[h, :, pl.ds(0, n)], e.astype(jnp.bfloat16),
                    preferred_element_type=jnp.float32)
        some = total > 0.0
        safe = jnp.where(some, total, 1.0)
        o = o * (1.0 / safe)
        lse = jnp.where(some, m + jnp.log2(safe), FLOOR)
        return o, lse

    lines = o_in.shape[3] - gw
    line_at = lax.broadcasted_iota(jnp.int32, (lines, tok), 0)

    def pack(lses):
        block = jnp.zeros((lines, tok), jnp.float32)
        for h, lse in enumerate(lses):
            rest = lse
            for j in range(3):
                piece = rest.astype(jnp.bfloat16).astype(jnp.float32)
                block = jnp.where(line_at == j * gh + h, piece, block)
                rest = rest - piece
        return block.astype(jnp.bfloat16)

    def unpack(block):
        b = block.astype(jnp.float32)
        return [b[h:h + 1] + b[gh + h:gh + h + 1] + b[2 * gh + h:2 * gh + h + 1]
                for h in range(gh)]

    def step_attend(g):
        for way in range(2):
            @pl.when(r_has[came[way]])
            def _(way=way):
                kv_copy(way, 0, g).wait_recv()
                kv_copy(way, 1, g).wait_recv()

        for h in range(gh):
            at = pl.ds(pl.multiple_of(g * gw + h * HD, HD), HD)
            vt[h] = v3[:, at].T

        for way in range(2):
            @pl.when(f_has[way])
            def _(way=way):
                d = 2 * came[way]
                for p in range(2):
                    qf_copy(came[way], p, g).wait_recv()
                for p in range(2):
                    bias = bias_in[p, came[way]]
                    lses = []
                    for h in range(gh):
                        o, lse = attend(p, d, h, g, bias)
                        o_out[way, p, g, pl.ds(h * HD, HD), :] = o.astype(jnp.bfloat16)
                        lses.append(lse)
                    o_out[way, p, g, pl.ds(gw, lines), :] = pack(lses)
                    of_copy(way, p, g).start()

        for p in range(2):
            bias = bias_own[0, 1] if p == 0 else bias_y[1]
            for h in range(gh):
                o, lse = attend(p, 1, h, g, bias)
                own[p, g, pl.ds(h * HD, HD), :] = o
                lse_own[p, g, pl.ds(h, 1), :] = lse

    def step_merge(g):
        for way in range(2):
            @pl.when(f_has[came[way]])
            def _(way=way):
                for p in range(2):
                    of_copy(way, p, g).wait_recv()
        for p in (1, 0):
            s0 = unpack(o_in[0, p, g, pl.ds(gw, lines), :])
            s1 = unpack(o_in[1, p, g, pl.ds(gw, lines), :])
            lses = []
            for h in range(gh):
                at = pl.ds(h * HD, HD)
                lo = lse_own[p, g, pl.ds(h, 1), :]
                top = jnp.maximum(jnp.maximum(s0[h], s1[h]), lo)
                w0, w1, wo = jnp.exp2(s0[h] - top), jnp.exp2(s1[h] - top), jnp.exp2(lo - top)
                z = w0 + w1 + wo
                inv = 1.0 / z
                o = (o_in[0, p, g, at, :].astype(jnp.float32) * (w0 * inv)
                     + o_in[1, p, g, at, :].astype(jnp.float32) * (w1 * inv)
                     + own[p, g, at, :] * (wo * inv))
                lse = top + jnp.log2(z)
                if p == 1:
                    y_out[g, at, :] = o.astype(jnp.bfloat16)
                    lses.append(lse)
                else:
                    own[0, g, at, :] = o
                    lse_own[0, g, pl.ds(h, 1), :] = lse
            if p == 1:
                y_out[g, pl.ds(gw, lines), :] = pack(lses)
                oy_copy(g).start()

    def step_project(g):
        oy_copy(g).wait_recv()
        s0 = unpack(y_in[g, pl.ds(gw, lines), :])
        parts = []
        for h in range(gh):
            at = pl.ds(h * HD, HD)
            lo = lse_own[0, g, pl.ds(h, 1), :]
            top = jnp.maximum(s0[h], lo)
            w0, wo = jnp.exp2(s0[h] - top), jnp.exp2(lo - top)
            inv = 1.0 / (w0 + wo)
            o = y_in[g, at, :].astype(jnp.float32) * (w0 * inv) + own[0, g, at, :] * (wo * inv)
            parts.append(o.T.astype(jnp.bfloat16))
        att = jnp.concatenate(parts, axis=1)

        @pl.when(g == 0)
        def _():
            w_copy.wait()

        rows = pl.ds(pl.multiple_of(g * gw, gw), gw)
        out_w = acc.shape[1]
        tile = 512 if out_w % 512 == 0 else out_w
        for c in range(out_w // tile):
            at = pl.ds(c * tile, tile)
            part = jnp.dot(att, w_v[rows, at], preferred_element_type=jnp.float32)

            @pl.when(g == 0)
            def _(part=part, at=at):
                acc[:, at] = part

            @pl.when(jnp.logical_and(g > 0, g < groups - 1))
            def _(part=part, at=at):
                acc[:, at] += part

            @pl.when(g == groups - 1)
            def _(part=part, at=at):
                out_ref[:, at] = ((acc[:, at] + part) * gate_ref[:, at]).astype(out_ref.dtype)

    @pl.loop(0, groups + 2)
    def _(i):
        @pl.when(i + 1 < groups)
        def _():
            pass_on(i + 1)

        @pl.when(i < groups)
        def _():
            step_attend(i)

        @pl.when(jnp.logical_and(i >= 1, i < groups + 1))
        def _():
            step_merge(i - 1)

        @pl.when(i >= 2)
        def _():
            step_project(i - 2)

    by_copy().wait_send()
    for way in range(2):
        @pl.when(f_has[way])
        def _(way=way):
            for p in range(2):
                bf_copy(way, p).wait_send()

    @pl.loop(0, groups)
    def _(g):
        qy_copy(g).wait_send()
        oy_copy(g).wait_send()
        for way in range(2):
            @pl.when(f_has[way])
            def _(way=way):
                for p in range(2):
                    qf_copy(way, p, g).wait_send()
                    of_copy(way, p, g).wait_send()

            @pl.when(r_has[way])
            def _(way=way):
                for which in range(2):
                    kv_copy(way, which, g).wait_send()


def local(nf, nr, queries, keys, values, window_mask, tile_valid, w_out, gate):
    frames, rows, columns, width = queries.shape
    tok = frames * rows * columns
    out_w = w_out.shape[1]
    heads = width // HD
    groups = GROUPS if heads % GROUPS == 0 else 1
    gw = width // groups
    gh = heads // groups
    lines = gw + 16 * (-(-3 * gh // 16))
    bf, f32 = jnp.bfloat16, jnp.float32
    hbm = pl.BlockSpec(memory_space=pl.ANY)
    smem = pl.BlockSpec(memory_space=pltpu.SMEM)
    vmem = pl.BlockSpec(memory_space=pltpu.VMEM)
    dma = pltpu.SemaphoreType.DMA
    out = pl.pallas_call(
        functools.partial(kernel, nf, nr, groups),
        out_shape=jax.ShapeDtypeStruct((tok, out_w), bf),
        in_specs=[hbm, hbm, hbm, smem, smem, hbm, vmem],
        out_specs=vmem,
        scratch_shapes=[
            pltpu.VMEM((3 * tok, width), bf),
            pltpu.VMEM((3 * tok, width), bf),
            pltpu.VMEM((gh, HD, 3 * tok), bf),
            pltpu.VMEM((2, 3, tok, width), bf),
            pltpu.VMEM((2, 3, 8, tok), f32),
            pltpu.VMEM((2, 2, 8, tok), f32),
            pltpu.VMEM((3, 8, tok), f32),
            pltpu.VMEM((2, 2, groups, lines, tok), bf),
            pltpu.VMEM((2, 2, groups, lines, tok), bf),
            pltpu.VMEM((2, groups, gw, tok), f32),
            pltpu.VMEM((2, groups, 8 * (-(-gh // 8)), tok), f32),
            pltpu.VMEM((groups, lines, tok), bf),
            pltpu.VMEM((groups, lines, tok), bf),
            pltpu.VMEM(w_out.shape, bf),
            pltpu.VMEM((tok, out_w), f32),
            dma((2, 2, groups)), dma((2, 2, groups)),
            dma((groups,)), dma((groups,)),
            dma((2, 2, groups)), dma((2, 2, groups)),
            dma((2, 2, groups)), dma((2, 2, groups)),
            dma((groups,)), dma((groups,)),
            dma, dma,
            dma((2, 2)), dma((2, 2)),
            dma((3,)), dma,
        ],
        compiler_params=pltpu.CompilerParams(
            collective_id=0, has_side_effects=True, vmem_limit_bytes=48 * 1024 * 1024),
    )(
        queries.reshape(tok, width), keys.reshape(tok, width), values.reshape(tok, width),
        window_mask, tile_valid, w_out, gate.reshape(1, out_w),
    )
    return out.reshape(frames, rows, columns, out_w)


def solution(mesh):
    split = P("frame", "row", None, None)
    nf, nr = mesh.shape["frame"], mesh.shape["row"]
    return jax.shard_map(
        functools.partial(local, nf, nr), mesh=mesh,
        in_specs=(split, split, split, split, P(), P(), P()), out_specs=split, check_vma=False,
    )
```
